32 devices in a mesh: space: 2 (over core), chan: 16 (over z, y, x).
Axes of the slice: x: 2, y: 2, z: 4, core: 2. Of those that a mesh axis runs over, the one named last changes fastest.
Arguments:
- acts: bfloat16 [256, 128, 4096], P('chan', 'space'), may hold values from -6 to 6
- w_point: bfloat16 [256, 256], replicated, may hold values from -0.375 to 0.375
- w_tap: bfloat16 [8, 256, 256], replicated, may hold values from -0.125 to 0.125
- grad_out: bfloat16 [256, 64, 1024], P('chan', 'space'), may hold values from -6 to 6
Outputs:
- out_map: bfloat16 [256, 64, 1024], P(None, ('space', 'chan'))
- d_acts: bfloat16 [256, 128, 4096], P(None, ('space', 'chan'))
- d_point: float32 [256, 256], P('chan', 'space')
- d_tap: float32 [8, 256, 256], P(None, 'chan', 'space')
The draws below stay inside these ranges and needn't reach their ends.
All inputs are finite; a program needn't handle non-finite values.
Results may differ from the reference program's by a relative error of at most 0.0049.
Values may be sent and summed in bfloat16 or wider, within the bound.
A program may use at most 128 MiB of HBM per device.

```python
import math
import jax
import jax.numpy as jnp
from jax import lax

C = 256
F = 256
H = 64
W = 64
ROWS = 128
IN_CELLS = 524288
OUT_CELLS = 65536


def levels(stream_key, shape, cuts, smallest, top_value):
    level, own = 1.0, jax.random.fold_in(stream_key, 6)
    for dim, shards_of in cuts:
        steps = jnp.exp(jax.random.uniform(jax.random.fold_in(own, dim), (shards_of,), jnp.float32, smallest / len(cuts), top_value / len(cuts)))
        level = level * jnp.repeat(steps, shape[dim] // shards_of).reshape([-1 if axis == dim else 1 for axis in range(len(shape))])
    return level


def centred(rng, shape, width, bound, split=(), kind=jnp.bfloat16):
    values = width * jax.random.normal(rng, shape, jnp.float32)
    if split:
        values = values * levels(rng, shape, split, -0.22, 0.18)
    return jnp.clip(values, -bound, bound).astype(kind)


def setup_inputs(seed: int = 0) -> dict:
    arg_keys = jax.random.split(jax.random.key(seed), 5)
    return {
        "acts": centred(arg_keys[0], (C, ROWS, H * W), 1.0, 6.0, ((0, 16), (1, 2))),
        "w_point": centred(arg_keys[1], (C, C), C ** -0.5, 0.375),
        "w_tap": centred(arg_keys[2], (8, C, F), (8 * C) ** -0.5, 0.125),
        "grad_out": centred(arg_keys[3], (F, ROWS // 2, H * W // 4), 1.0, 6.0, ((0, 16), (1, 2))),
    }


def gelu_tanh(value):
    return jax.nn.gelu(value, approximate=True)

def block_pass(inputs, grad_cells, w_point, w_tap):
    row_count = inputs.shape[1]
    pre_act = jnp.einsum('cd,crp->drp', w_point.astype(jnp.float32), inputs.astype(jnp.float32))
    hidden_full, gelu_back = jax.vjp(gelu_tanh, pre_act)
    hidden = hidden_full.astype(jnp.bfloat16)
    hidden_cube = hidden.astype(jnp.float32).reshape(C, row_count // 2, 2, H // 2, 2, W // 2, 2)
    tap_weights = w_tap.astype(jnp.float32).reshape(2, 2, 2, C, F)
    output = jnp.einsum('abedf,dqaibje->fqij', tap_weights, hidden_cube)
    output = output.reshape(F, row_count // 2, H // 2 * (W // 2)).astype(jnp.bfloat16)
    grad_cube = grad_cells.astype(jnp.float32).reshape(F, row_count // 2, H // 2, W // 2)
    tap_part = jnp.einsum('dqaibje,fqij->abedf', hidden_cube, grad_cube).reshape(8, C, F)
    dhidden = jnp.einsum('abedf,fqij->dqaibje', tap_weights, grad_cube).reshape(C, row_count, H * W)
    pre_grad = gelu_back(dhidden)[0].astype(jnp.bfloat16)
    point_part = jnp.einsum('crp,drp->cd', inputs.astype(jnp.float32), pre_grad.astype(jnp.float32))
    d_inputs = jnp.einsum('cd,drp->crp', w_point.astype(jnp.float32), pre_grad.astype(jnp.float32)).astype(jnp.bfloat16)
    return (output, d_inputs, point_part, tap_part)

def reference(acts, w_point, w_tap, grad_out):
    row_total = acts.shape[1]
    block_rows = 8
    block_count = row_total // block_rows

    def block_step(totals, pair_index):
        row_start = pair_index * block_rows
        inputs = lax.dynamic_slice_in_dim(acts, row_start, block_rows, 1)
        grad_cells = lax.dynamic_slice_in_dim(grad_out, pair_index * (block_rows // 2), block_rows // 2, 1)
        output, d_inputs, point_part, tap_part = block_pass(inputs, grad_cells, w_point, w_tap)
        return ((totals[0] + point_part, totals[1] + tap_part), (output, d_inputs))
    start_totals = (jnp.zeros((C, C), jnp.float32), jnp.zeros((8, C, F), jnp.float32))
    totals, stacked = lax.scan(block_step, start_totals, jnp.arange(block_count, dtype=jnp.int32))
    out_map = jnp.transpose(stacked[0], (1, 0, 2, 3)).reshape(F, row_total // 2, H // 2 * (W // 2))
    d_acts = jnp.transpose(stacked[1], (1, 0, 2, 3)).reshape(C, row_total, H * W)
    d_point = totals[0] * (1.0 / math.sqrt(IN_CELLS))
    d_tap = totals[1] * (1.0 / math.sqrt(OUT_CELLS))
    return (out_map, d_acts, d_point, d_tap)
```

```python
import functools
import math

import jax
import jax.numpy as jnp
from jax import lax
from jax.experimental import pallas as pl
from jax.experimental.pallas import tpu as pltpu
from jax.sharding import PartitionSpec as P

H = 64
W = 64
BLOCK = 8 * W
CHUNK = 2 * BLOCK
ROOT = math.sqrt(2.0 / math.pi)
CUBIC = 0.044715


def dot(a, b):
    return lax.dot_general(a, b, (((1,), (0,)), ((), ())), preferred_element_type=jnp.float32)


def dot_nt(a, b):
    return lax.dot_general(a, b, (((1,), (1,)), ((), ())), preferred_element_type=jnp.float32)


def tap_order(position):
    quarter = BLOCK // 4
    u = position // quarter
    rest = position % quarter
    i = rest // (W // 2)
    j = rest % (W // 2)
    return (2 * i + u // 2) * W + 2 * j + u % 2


def kernel(
    spaces, chans, planes, in_scale, out_scale,
    xs, gs, wp, wt,
    out_o, da_o, dtap_o, dpoint_o,
    recv, recvg, acc, recv_a, send_b, recv_b, taps, dtaps, order, back, wt_t, wp_t,
    send_sem, g_send, recv_sem, g_recv, a_send, a_recv, b_send, b_recv,
):
    me_s, me_c = lax.axis_index("space"), lax.axis_index("chan")
    width = xs.shape[1]
    pairs = planes // 2
    parts = xs.shape[2] // CHUNK
    out_cells = CHUNK // 4
    filters = acc.shape[3]

    barrier = pltpu.get_barrier_semaphore()
    for o in range(1, chans):
        pl.semaphore_signal(barrier, inc=1, device_id={"chan": lax.rem(me_c + o, chans)})
    for o in range(1, spaces):
        pl.semaphore_signal(barrier, inc=1, device_id={"space": lax.rem(me_s + o, spaces)})
    pl.semaphore_wait(barrier, chans + spaces - 2)

    mine = pl.ds(pl.multiple_of(me_c * width, width), width)

    def remote(src, dst, ssem, rsem, device):
        return pltpu.make_async_remote_copy(
            src_ref=src, dst_ref=dst, send_sem=ssem, recv_sem=rsem, device_id=device)

    def g_block(peer):
        return gs.at[pl.ds(peer * pairs, pairs)]

    def x_block(peer, k):
        lanes = pl.ds(pl.multiple_of((k % parts) * CHUNK, CHUNK), CHUNK)
        return xs.at[pl.ds(peer * planes + 2 * (k // parts), 2), :, lanes]

    pltpu.make_async_copy(g_block(me_c), recvg.at[:, mine], g_recv).start()

    @pl.loop(1, chans)
    def _(o):
        peer = lax.rem(me_c + o, chans)
        remote(g_block(peer), recvg.at[:, mine], g_send, g_recv, {"chan": peer}).start()

    @pl.loop(0, pairs * parts)
    def _(k):
        pltpu.make_async_copy(x_block(me_c, k), recv.at[k, :, mine], recv_sem.at[k]).start()

        @pl.loop(1, chans)
        def _(o):
            peer = lax.rem(me_c + o, chans)
            remote(x_block(peer, k), recv.at[k, :, mine], send_sem, recv_sem.at[k], {"chan": peer}).start()

    acc[...] = jnp.zeros_like(acc)
    rows = lax.broadcasted_iota(jnp.int32, (BLOCK, BLOCK), 0)
    cols = lax.broadcasted_iota(jnp.int32, (BLOCK, BLOCK), 1)
    order[...] = jnp.where(rows == tap_order(cols), 1.0, 0.0).astype(jnp.bfloat16)
    back[...] = jnp.where(cols == tap_order(rows), 1.0, 0.0).astype(jnp.bfloat16)
    wp_t[...] = wp[...].astype(jnp.float32).T.astype(jnp.bfloat16)

    @pl.loop(0, 8)
    def _(t):
        wt_t[t] = wt[t].astype(jnp.float32).T.astype(jnp.bfloat16)

    def add_term(slot, term):
        for s in range(spaces):
            acc[s, slot] += term[:, s * filters:(s + 1) * filters]

    pltpu.make_async_copy(recvg, recvg, g_recv).wait()

    @pl.loop(0, pairs * parts)
    def _(k):
        pltpu.make_async_copy(recv.at[k], recv.at[k], recv_sem.at[k]).wait()
        q, part = k // parts, k % parts
        quarter = BLOCK // 4
        for a in range(2):
            for h in range(2):
                moved = dot(recv[k, a, :, h * BLOCK:(h + 1) * BLOCK], order[...]).astype(jnp.bfloat16)
                for u in range(4):
                    taps[4 * a + u, :, h * quarter:(h + 1) * quarter] = moved[:, u * quarter:(u + 1) * quarter]
        g_lanes = pl.ds(pl.multiple_of(part * out_cells, out_cells), out_cells)
        g = recvg[q, :, g_lanes]
        out = jnp.zeros((wt.shape[2], out_cells), jnp.float32)
        for t in range(8):
            x = taps[t]
            pre = dot(wp_t[...], x)
            dh = dot(wt[t], g)
            square = pre * pre
            th = jnp.tanh(ROOT * pre * (1.0 + CUBIC * square))
            half = 0.5 * (1.0 + th)
            hidden = (pre * half).astype(jnp.bfloat16)
            slope = half + (0.5 * ROOT) * pre * (1.0 - th * th) * (1.0 + 3.0 * CUBIC * square)
            grad = (dh * slope).astype(jnp.bfloat16)
            out += dot(wt_t[t], hidden)
            add_term(t, dot_nt(hidden, g))
            add_term(8, dot_nt(x, grad))
            d_in = dot(wp[...], grad).astype(jnp.bfloat16)
            for h in range(2):
                dtaps[t // 4, h, :, (t % 4) * quarter:(t % 4 + 1) * quarter] = d_in[:, h * quarter:(h + 1) * quarter]
        out_o[q, :, g_lanes] = out.astype(jnp.bfloat16)
        for a in range(2):
            for h in range(2):
                lanes = pl.ds(pl.multiple_of(part * CHUNK + h * BLOCK, BLOCK), BLOCK)
                da_o[2 * q + a, :, lanes] = dot(dtaps[a, h], back[...]).astype(jnp.bfloat16)

    copies = []
    for o in range(1, spaces):
        other = lax.rem(me_s + o, spaces)
        copy = remote(acc.at[other], recv_a.at[me_s], a_send.at[o - 1], a_recv.at[o - 1], {"space": other})
        copy.start()
        copies.append(copy)
    for copy in copies:
        copy.wait()

    def reduced(c):
        at = pl.ds(pl.multiple_of(c * width, width), width)
        total = acc[me_s, :, at, :]
        for o in range(1, spaces):
            total += recv_a[lax.rem(me_s + o, spaces), :, at, :]
        return total.astype(jnp.bfloat16)

    @pl.loop(1, chans)
    def _(o):
        peer = lax.rem(me_c + o, chans)
        send_b[peer] = reduced(peer)
        remote(send_b.at[peer], recv_b.at[me_c], b_send, b_recv, {"chan": peer}).start()

    send_b[me_c] = reduced(me_c)
    pltpu.make_async_copy(send_b.at[me_c], recv_b.at[me_c], b_recv).start()
    pltpu.make_async_copy(recv_b, recv_b, b_recv).wait()
    total = recv_b[0].astype(jnp.float32)
    for c in range(1, chans):
        total += recv_b[c].astype(jnp.float32)
    dtap_o[...] = total[:8] * out_scale
    dpoint_o[...] = total[8] * in_scale

    sent = xs.at[pl.ds(0, planes * (chans - 1))]
    pltpu.make_async_copy(sent, sent, send_sem).wait()
    sent_g = gs.at[pl.ds(0, pairs * (chans - 1))]
    pltpu.make_async_copy(sent_g, sent_g, g_send).wait()
    sent_b = send_b.at[pl.ds(0, chans - 1)]
    pltpu.make_async_copy(sent_b, sent_b, b_send).wait()


def shards(acts, w_point, w_tap, grad_out):
    spaces = lax.axis_size("space")
    chans = lax.axis_size("chan")
    width, rows, cells = acts.shape
    planes = rows // chans
    channels = width * chans
    filters = w_tap.shape[2]
    in_cells = rows * spaces * H * W
    xs = jnp.transpose(acts, (1, 0, 2))
    gs = jnp.transpose(grad_out, (1, 0, 2))
    chunks = (planes // 2) * (cells // CHUNK)
    bf16, f32 = jnp.bfloat16, jnp.float32
    vmem = pl.BlockSpec(memory_space=pltpu.VMEM)
    own = filters // spaces
    out, da, d_tap, d_point = pl.pallas_call(
        functools.partial(kernel, spaces, chans, planes, 1.0 / math.sqrt(in_cells), 1.0 / math.sqrt(in_cells // 8)),
        out_shape=(
            jax.ShapeDtypeStruct((planes // 2, filters, cells // 4), bf16),
            jax.ShapeDtypeStruct((planes, channels, cells), bf16),
            jax.ShapeDtypeStruct((8, width, own), f32),
            jax.ShapeDtypeStruct((width, own), f32),
        ),
        in_specs=[pl.BlockSpec(memory_space=pl.ANY)] * 2 + [vmem] * 2,
        out_specs=(vmem,) * 4,
        scratch_shapes=[
            pltpu.VMEM((chunks, 2, channels, CHUNK), bf16),
            pltpu.VMEM((planes // 2, filters, cells // 4), bf16),
            pltpu.VMEM((spaces, 9, channels, own), f32),
            pltpu.VMEM((spaces, 9, channels, own), f32),
            pltpu.VMEM((chans, 9, width, own), bf16),
            pltpu.VMEM((chans, 9, width, own), bf16),
            pltpu.VMEM((8, channels, CHUNK // 4), bf16),
            pltpu.VMEM((2, 2, channels, BLOCK), bf16),
            pltpu.VMEM((BLOCK, BLOCK), bf16),
            pltpu.VMEM((BLOCK, BLOCK), bf16),
            pltpu.VMEM((8, filters, channels), bf16),
            pltpu.VMEM((channels, channels), bf16),
            pltpu.SemaphoreType.DMA,
            pltpu.SemaphoreType.DMA,
            pltpu.SemaphoreType.DMA((chunks,)),
            pltpu.SemaphoreType.DMA,
            pltpu.SemaphoreType.DMA((max(spaces - 1, 1),)),
            pltpu.SemaphoreType.DMA((max(spaces - 1, 1),)),
            pltpu.SemaphoreType.DMA,
            pltpu.SemaphoreType.DMA,
        ],
        compiler_params=pltpu.CompilerParams(
            collective_id=0, has_side_effects=True, vmem_limit_bytes=58 * 2**20
        ),
        cost_estimate=pl.CostEstimate(flops=24 * 10**9, bytes_accessed=30 * 10**6, transcendentals=4 * 10**6),
    )(xs, gs, w_point, w_tap)
    return (jnp.transpose(out, (1, 0, 2)), jnp.transpose(da, (1, 0, 2)), d_point, d_tap)


def solution(mesh):
    placed = (P("chan", "space", None), P(), P(), P("chan", "space", None))
    return jax.shard_map(
        shards,
        mesh=mesh,
        in_specs=placed,
        out_specs=(
            P(None, ("space", "chan"), None),
            P(None, ("space", "chan"), None),
            P("chan", "space"),
            P(None, "chan", "space"),
        ),
        check_vma=False,
    )
```

```python
import functools
import math

import jax
import jax.numpy as jnp
from jax import lax
from jax.experimental import pallas as pl
from jax.experimental.pallas import tpu as pltpu
from jax.sharding import PartitionSpec as P

H = 64
W = 64
BLOCK = 8 * W
CHUNK = 2 * BLOCK
ROOT = math.sqrt(2.0 / math.pi)
CUBIC = 0.044715


def dot(a, b):
    return lax.dot_general(a, b, (((1,), (0,)), ((), ())), preferred_element_type=jnp.float32)


def dot_nt(a, b):
    return lax.dot_general(a, b, (((1,), (1,)), ((), ())), preferred_element_type=jnp.float32)


def tap_order(position):
    quarter = BLOCK // 4
    u = position // quarter
    rest = position % quarter
    i = rest // (W // 2)
    j = rest % (W // 2)
    return (2 * i + u // 2) * W + 2 * j + u % 2


def kernel(
    spaces, chans, planes, in_scale, out_scale,
    acts, grad_out, wp, wt,
    out_o, da_o, dtap_o, dpoint_o,
    xs, gs, stage, g_stage, da_v,
    recv, recvg, acc, recv_a, send_b, recv_b, taps, dtaps, grads, hid, order, back, wt_t, wp_t,
    load_sem, g_load, da_sem, send_sem, g_send, recv_sem, g_recv, a_send, a_recv, b_send, b_recv,
):
    me_s, me_c = lax.axis_index("space"), lax.axis_index("chan")
    width = acts.shape[0]
    pairs = planes // 2
    parts = acts.shape[2] // CHUNK

    def load(part, slot):
        lanes = pl.ds(pl.multiple_of(part * CHUNK, CHUNK), CHUNK)
        return pltpu.make_async_copy(acts.at[:, :, lanes], stage.at[slot], load_sem.at[slot])

    g_copy = pltpu.make_async_copy(grad_out, g_stage, g_load)
    g_copy.start()
    load(0, 0).start()

    def swap(src, dst):
        @pl.loop(0, src.shape[2] // 128)
        def _(lane):
            lanes = pl.ds(pl.multiple_of(lane * 128, 128), 128)
            for r in range(0, src.shape[1], 16):
                piece = src[:, r:r + 16, lanes].astype(jnp.float32)
                dst[r:r + 16, :, lanes] = jnp.swapaxes(piece, 0, 1).astype(jnp.bfloat16)

    out_cells = CHUNK // 4
    filters = acc.shape[3]

    barrier = pltpu.get_barrier_semaphore()
    for o in range(1, chans):
        pl.semaphore_signal(barrier, inc=1, device_id={"chan": lax.rem(me_c + o, chans)})
    for o in range(1, spaces):
        pl.semaphore_signal(barrier, inc=1, device_id={"space": lax.rem(me_s + o, spaces)})
    pl.semaphore_wait(barrier, chans + spaces - 2)

    mine = pl.ds(pl.multiple_of(me_c * width, width), width)

    def remote(src, dst, ssem, rsem, device):
        return pltpu.make_async_remote_copy(
            src_ref=src, dst_ref=dst, send_sem=ssem, recv_sem=rsem, device_id=device)

    def g_block(peer):
        return gs.at[pl.ds(peer * pairs, pairs)]

    def x_block(peer, k):
        return xs.at[k // pairs, pl.ds(peer * planes + 2 * (k % pairs), 2)]

    g_copy.wait()
    swap(g_stage, gs)
    pltpu.make_async_copy(g_block(me_c), recvg.at[:, mine], g_recv).start()

    @pl.loop(1, chans)
    def _(o):
        peer = lax.rem(me_c + o, chans)
        remote(g_block(peer), recvg.at[:, mine], g_send, g_recv, {"chan": peer}).start()

    @pl.loop(0, parts)
    def _(part):
        slot = part % 2

        @pl.when(part + 1 < parts)
        def _():
            load(part + 1, (part + 1) % 2).start()

        load(part, slot).wait()
        swap(stage.at[slot], xs.at[part])

        @pl.loop(0, pairs)
        def _(q):
            k = part * pairs + q
            pltpu.make_async_copy(x_block(me_c, k), recv.at[k, :, mine], recv_sem.at[k]).start()

            @pl.loop(1, chans)
            def _(o):
                peer = lax.rem(me_c + o, chans)
                remote(x_block(peer, k), recv.at[k, :, mine], send_sem, recv_sem.at[k], {"chan": peer}).start()

    acc[...] = jnp.zeros_like(acc)
    rows = lax.broadcasted_iota(jnp.int32, (BLOCK, BLOCK), 0)
    cols = lax.broadcasted_iota(jnp.int32, (BLOCK, BLOCK), 1)
    order[...] = jnp.where(rows == tap_order(cols), 1.0, 0.0).astype(jnp.bfloat16)
    back[...] = jnp.where(cols == tap_order(rows), 1.0, 0.0).astype(jnp.bfloat16)
    wp_t[...] = wp[...].astype(jnp.float32).T.astype(jnp.bfloat16)

    @pl.loop(0, 8)
    def _(t):
        wt_t[:, pl.ds(pl.multiple_of(t * wp.shape[0], 128), wp.shape[0])] = wt[t].astype(jnp.float32).T.astype(jnp.bfloat16)

    def add_term(slot, term):
        for s in range(spaces):
            acc[s, slot] += term[:, s * filters:(s + 1) * filters]

    pltpu.make_async_copy(recvg, recvg, g_recv).wait()

    @pl.loop(0, pairs * parts)
    def _(k):
        pltpu.make_async_copy(recv.at[k], recv.at[k], recv_sem.at[k]).wait()
        q, part = k % pairs, k // pairs
        quarter = BLOCK // 4
        for a in range(2):
            for h in range(2):
                moved = dot(recv[k, a, :, h * BLOCK:(h + 1) * BLOCK], order[...]).astype(jnp.bfloat16)
                for u in range(4):
                    at = (4 * a + u) * out_cells + h * quarter
                    taps[:, at:at + quarter] = moved[:, u * quarter:(u + 1) * quarter]
        g_lanes = pl.ds(pl.multiple_of(part * out_cells, out_cells), out_cells)
        g = recvg[q, :, g_lanes]
        for t in range(8):
            here = slice(t * out_cells, (t + 1) * out_cells)
            x = taps[:, here]
            pre = dot(wp_t[...], x)
            dh = dot(wt[t], g)
            square = pre * pre
            th = jnp.tanh(ROOT * pre * (1.0 + CUBIC * square))
            half = 0.5 * (1.0 + th)
            hidden = (pre * half).astype(jnp.bfloat16)
            slope = half + (0.5 * ROOT) * pre * (1.0 - th * th) * (1.0 + 3.0 * CUBIC * square)
            grad = (dh * slope).astype(jnp.bfloat16)
            hid[t * hidden.shape[0]:(t + 1) * hidden.shape[0], :] = hidden
            grads[:, here] = grad
            add_term(t, dot_nt(hidden, g))
            d_in = dot(wp[...], grad).astype(jnp.bfloat16)
            for h in range(2):
                dtaps[t // 4, h, :, (t % 4) * quarter:(t % 4 + 1) * quarter] = d_in[:, h * quarter:(h + 1) * quarter]
        add_term(8, dot_nt(taps[...], grads[...]))
        out_o[q, :, g_lanes] = dot(wt_t[...], hid[...]).astype(jnp.bfloat16)
        for a in range(2):
            for h in range(2):
                lanes = pl.ds(pl.multiple_of(part * CHUNK + h * BLOCK, BLOCK), BLOCK)
                da_v[2 * q + a, :, lanes] = dot(dtaps[a, h], back[...]).astype(jnp.bfloat16)
        block = (pl.ds(2 * q, 2), slice(None), pl.ds(pl.multiple_of(part * CHUNK, CHUNK), CHUNK))
        pltpu.make_async_copy(da_v.at[block], da_o.at[block], da_sem).start()

    copies = []
    for o in range(1, spaces):
        other = lax.rem(me_s + o, spaces)
        copy = remote(acc.at[other], recv_a.at[me_s], a_send.at[o - 1], a_recv.at[o - 1], {"space": other})
        copy.start()
        copies.append(copy)
    for copy in copies:
        copy.wait()

    def reduced(c):
        at = pl.ds(pl.multiple_of(c * width, width), width)
        total = acc[me_s, :, at, :]
        for o in range(1, spaces):
            total += recv_a[lax.rem(me_s + o, spaces), :, at, :]
        return total.astype(jnp.bfloat16)

    @pl.loop(1, chans)
    def _(o):
        peer = lax.rem(me_c + o, chans)
        send_b[peer] = reduced(peer)
        remote(send_b.at[peer], recv_b.at[me_c], b_send, b_recv, {"chan": peer}).start()

    send_b[me_c] = reduced(me_c)
    pltpu.make_async_copy(send_b.at[me_c], recv_b.at[me_c], b_recv).start()
    pltpu.make_async_copy(recv_b, recv_b, b_recv).wait()
    total = recv_b[0].astype(jnp.float32)
    for c in range(1, chans):
        total += recv_b[c].astype(jnp.float32)
    dtap_o[...] = total[:8] * out_scale
    dpoint_o[...] = total[8] * in_scale

    sent = xs.at[:, pl.ds(0, planes * (chans - 1))]
    pltpu.make_async_copy(sent, sent, send_sem).wait()
    sent_g = gs.at[pl.ds(0, pairs * (chans - 1))]
    pltpu.make_async_copy(sent_g, sent_g, g_send).wait()
    pltpu.make_async_copy(da_v, da_o, da_sem).wait()
    sent_b = send_b.at[pl.ds(0, chans - 1)]
    pltpu.make_async_copy(sent_b, sent_b, b_send).wait()


def shards(acts, w_point, w_tap, grad_out):
    spaces = lax.axis_size("space")
    chans = lax.axis_size("chan")
    width, rows, cells = acts.shape
    planes = rows // chans
    channels = width * chans
    filters = w_tap.shape[2]
    in_cells = rows * spaces * H * W
    chunks = (planes // 2) * (cells // CHUNK)
    bf16, f32 = jnp.bfloat16, jnp.float32
    vmem = pl.BlockSpec(memory_space=pltpu.VMEM)
    own = filters // spaces
    out, da, d_tap, d_point = pl.pallas_call(
        functools.partial(kernel, spaces, chans, planes, 1.0 / math.sqrt(in_cells), 1.0 / math.sqrt(in_cells // 8)),
        out_shape=(
            jax.ShapeDtypeStruct((planes // 2, filters, cells // 4), bf16),
            jax.ShapeDtypeStruct((planes, channels, cells), bf16),
            jax.ShapeDtypeStruct((8, width, own), f32),
            jax.ShapeDtypeStruct((width, own), f32),
        ),
        in_specs=[pl.BlockSpec(memory_space=pl.ANY)] * 2 + [vmem] * 2,
        out_specs=(vmem, pl.BlockSpec(memory_space=pl.ANY), vmem, vmem),
        scratch_shapes=[
            pltpu.VMEM((cells // CHUNK, rows, width, CHUNK), bf16),
            pltpu.VMEM((rows // 2, width, cells // 4), bf16),
            pltpu.VMEM((2, width, rows, CHUNK), bf16),
            pltpu.VMEM((width, rows // 2, cells // 4), bf16),
            pltpu.VMEM((planes, channels, cells), bf16),
            pltpu.VMEM((chunks, 2, channels, CHUNK), bf16),
            pltpu.VMEM((planes // 2, filters, cells // 4), bf16),
            pltpu.VMEM((spaces, 9, channels, own), f32),
            pltpu.VMEM((spaces, 9, channels, own), f32),
            pltpu.VMEM((chans, 9, width, own), bf16),
            pltpu.VMEM((chans, 9, width, own), bf16),
            pltpu.VMEM((channels, 2 * CHUNK), bf16),
            pltpu.VMEM((2, 2, channels, BLOCK), bf16),
            pltpu.VMEM((channels, 2 * CHUNK), bf16),
            pltpu.VMEM((8 * channels, CHUNK // 4), bf16),
            pltpu.VMEM((BLOCK, BLOCK), bf16),
            pltpu.VMEM((BLOCK, BLOCK), bf16),
            pltpu.VMEM((filters, 8 * channels), bf16),
            pltpu.VMEM((channels, channels), bf16),
            pltpu.SemaphoreType.DMA((2,)),
            pltpu.SemaphoreType.DMA,
            pltpu.SemaphoreType.DMA,
            pltpu.SemaphoreType.DMA,
            pltpu.SemaphoreType.DMA,
            pltpu.SemaphoreType.DMA((chunks,)),
            pltpu.SemaphoreType.DMA,
            pltpu.SemaphoreType.DMA((max(spaces - 1, 1),)),
            pltpu.SemaphoreType.DMA((max(spaces - 1, 1),)),
            pltpu.SemaphoreType.DMA,
            pltpu.SemaphoreType.DMA,
        ],
        compiler_params=pltpu.CompilerParams(
            collective_id=0, has_side_effects=True, vmem_limit_bytes=58 * 2**20
        ),
        cost_estimate=pl.CostEstimate(flops=24 * 10**9, bytes_accessed=30 * 10**6, transcendentals=4 * 10**6),
    )(acts, grad_out, w_point, w_tap)
    return (jnp.transpose(out, (1, 0, 2)), jnp.transpose(da, (1, 0, 2)), d_point, d_tap)


def solution(mesh):
    placed = (P("chan", "space", None), P(), P(), P("chan", "space", None))
    return jax.shard_map(
        shards,
        mesh=mesh,
        in_specs=placed,
        out_specs=(
            P(None, ("space", "chan"), None),
            P(None, ("space", "chan"), None),
            P("chan", "space"),
            P(None, "chan", "space"),
        ),
        check_vma=False,
    )
```

```python
import functools
import math

import jax
import jax.numpy as jnp
from jax import lax
from jax.experimental import pallas as pl
from jax.experimental.pallas import tpu as pltpu
from jax.sharding import PartitionSpec as P

H = 64
W = 64
BLOCK = 8 * W
CHUNK = 2 * BLOCK
ROOT = math.sqrt(2.0 / math.pi)
CUBIC = 0.044715


def dot(a, b):
    return lax.dot_general(a, b, (((1,), (0,)), ((), ())), preferred_element_type=jnp.float32)


def dot_nt(a, b):
    return lax.dot_general(a, b, (((1,), (1,)), ((), ())), preferred_element_type=jnp.float32)


def tap_order(position):
    quarter = BLOCK // 4
    u = position // quarter
    rest = position % quarter
    i = rest // (W // 2)
    j = rest % (W // 2)
    return (2 * i + u // 2) * W + 2 * j + u % 2


def kernel(
    spaces, chans, planes, in_scale, out_scale,
    acts, grad_out, wp, wt,
    out_o, da_o, dtap_o, dpoint_o,
    xs, gs, stage, g_stage, da_v,
    recv, recvg, acc, recv_a, send_b, recv_b, taps, dtaps, grads, hid, order, back, wt_t, wp_t,
    load_sem, g_load, da_sem, send_sem, g_send, recv_sem, g_recv, a_send, a_recv, b_send, b_recv,
):
    me_s, me_c = lax.axis_index("space"), lax.axis_index("chan")
    width = acts.shape[0]
    pairs = planes // 2
    stride = next(n for n in range(chans // 2 - 1, 0, -1) if math.gcd(n, chans) == 1)
    parts = acts.shape[2] // CHUNK

    def load(part, slot):
        lanes = pl.ds(pl.multiple_of(part * CHUNK, CHUNK), CHUNK)
        return pltpu.make_async_copy(acts.at[:, :, lanes], stage.at[slot], load_sem.at[slot])

    g_copy = pltpu.make_async_copy(grad_out, g_stage, g_load)
    g_copy.start()
    load(0, 0).start()

    def swap(src, dst):
        @pl.loop(0, src.shape[2] // 128)
        def _(lane):
            lanes = pl.ds(pl.multiple_of(lane * 128, 128), 128)
            for r in range(0, src.shape[1], 16):
                piece = src[:, r:r + 16, lanes].astype(jnp.float32)
                dst[r:r + 16, :, lanes] = jnp.swapaxes(piece, 0, 1).astype(jnp.bfloat16)

    out_cells = CHUNK // 4
    filters = acc.shape[3]

    barrier = pltpu.get_barrier_semaphore()
    for o in range(1, chans):
        pl.semaphore_signal(barrier, inc=1, device_id={"chan": lax.rem(me_c + o, chans)})
    for o in range(1, spaces):
        pl.semaphore_signal(barrier, inc=1, device_id={"space": lax.rem(me_s + o, spaces)})
    pl.semaphore_wait(barrier, chans + spaces - 2)

    mine = pl.ds(pl.multiple_of(me_c * width, width), width)

    def remote(src, dst, ssem, rsem, device):
        return pltpu.make_async_remote_copy(
            src_ref=src, dst_ref=dst, send_sem=ssem, recv_sem=rsem, device_id=device)

    def g_block(peer):
        return gs.at[pl.ds(peer * pairs, pairs)]

    def x_block(peer, k):
        return xs.at[k // pairs, pl.ds(peer * planes + 2 * (k % pairs), 2)]

    g_copy.wait()
    swap(g_stage, gs)
    pltpu.make_async_copy(g_block(me_c), recvg.at[:, mine], g_recv).start()

    @pl.loop(1, chans)
    def _(o):
        peer = lax.rem(me_c + o, chans)
        remote(g_block(peer), recvg.at[:, mine], g_send, g_recv, {"chan": peer}).start()

    @pl.loop(0, parts)
    def _(part):
        slot = part % 2

        @pl.when(part + 1 < parts)
        def _():
            load(part + 1, (part + 1) % 2).start()

        load(part, slot).wait()
        swap(stage.at[slot], xs.at[part])

        @pl.loop(0, pairs)
        def _(q):
            k = part * pairs + q
            pltpu.make_async_copy(x_block(me_c, k), recv.at[k, :, mine], recv_sem.at[k]).start()

            @pl.loop(1, chans)
            def _(o):
                peer = lax.rem(me_c + stride * o, chans)
                remote(x_block(peer, k), recv.at[k, :, mine], send_sem, recv_sem.at[k], {"chan": peer}).start()

    acc[...] = jnp.zeros_like(acc)
    rows = lax.broadcasted_iota(jnp.int32, (BLOCK, BLOCK), 0)
    cols = lax.broadcasted_iota(jnp.int32, (BLOCK, BLOCK), 1)
    order[...] = jnp.where(rows == tap_order(cols), 1.0, 0.0).astype(jnp.bfloat16)
    back[...] = jnp.where(cols == tap_order(rows), 1.0, 0.0).astype(jnp.bfloat16)
    wp_t[...] = wp[...].astype(jnp.float32).T.astype(jnp.bfloat16)

    @pl.loop(0, 8)
    def _(t):
        wt_t[:, pl.ds(pl.multiple_of(t * wp.shape[0], 128), wp.shape[0])] = wt[t].astype(jnp.float32).T.astype(jnp.bfloat16)

    def add_term(slot, term):
        for s in range(spaces):
            acc[s, slot] += term[:, s * filters:(s + 1) * filters]

    pltpu.make_async_copy(recvg, recvg, g_recv).wait()

    @pl.loop(0, pairs * parts)
    def _(k):
        pltpu.make_async_copy(recv.at[k], recv.at[k], recv_sem.at[k]).wait()
        q, part = k % pairs, k // pairs
        quarter = BLOCK // 4
        for a in range(2):
            for h in range(2):
                moved = dot(recv[k, a, :, h * BLOCK:(h + 1) * BLOCK], order[...]).astype(jnp.bfloat16)
                for u in range(4):
                    at = (4 * a + u) * out_cells + h * quarter
                    taps[:, at:at + quarter] = moved[:, u * quarter:(u + 1) * quarter]
        g_lanes = pl.ds(pl.multiple_of(part * out_cells, out_cells), out_cells)
        g = recvg[q, :, g_lanes]
        for t in range(8):
            here = slice(t * out_cells, (t + 1) * out_cells)
            x = taps[:, here]
            pre = dot(wp_t[...], x)
            dh = dot(wt[t], g)
            square = pre * pre
            th = jnp.tanh(ROOT * pre * (1.0 + CUBIC * square))
            half = 0.5 * (1.0 + th)
            hidden = (pre * half).astype(jnp.bfloat16)
            slope = half + (0.5 * ROOT) * pre * (1.0 - th * th) * (1.0 + 3.0 * CUBIC * square)
            grad = (dh * slope).astype(jnp.bfloat16)
            hid[t * hidden.shape[0]:(t + 1) * hidden.shape[0], :] = hidden
            grads[:, here] = grad
            add_term(t, dot_nt(hidden, g))
            d_in = dot(wp[...], grad).astype(jnp.bfloat16)
            for h in range(2):
                dtaps[t // 4, h, :, (t % 4) * quarter:(t % 4 + 1) * quarter] = d_in[:, h * quarter:(h + 1) * quarter]
        add_term(8, dot_nt(taps[...], grads[...]))
        out_o[q, :, g_lanes] = dot(wt_t[...], hid[...]).astype(jnp.bfloat16)
        for a in range(2):
            for h in range(2):
                lanes = pl.ds(pl.multiple_of(part * CHUNK + h * BLOCK, BLOCK), BLOCK)
                da_v[2 * q + a, :, lanes] = dot(dtaps[a, h], back[...]).astype(jnp.bfloat16)
        block = (pl.ds(2 * q, 2), slice(None), pl.ds(pl.multiple_of(part * CHUNK, CHUNK), CHUNK))
        pltpu.make_async_copy(da_v.at[block], da_o.at[block], da_sem).start()

    copies = []
    for o in range(1, spaces):
        other = lax.rem(me_s + o, spaces)
        copy = remote(acc.at[other], recv_a.at[me_s], a_send.at[o - 1], a_recv.at[o - 1], {"space": other})
        copy.start()
        copies.append(copy)
    for copy in copies:
        copy.wait()

    def reduced(c):
        at = pl.ds(pl.multiple_of(c * width, width), width)
        total = acc[me_s, :, at, :]
        for o in range(1, spaces):
            total += recv_a[lax.rem(me_s + o, spaces), :, at, :]
        return total.astype(jnp.bfloat16)

    @pl.loop(1, chans)
    def _(o):
        peer = lax.rem(me_c + o, chans)
        send_b[peer] = reduced(peer)
        remote(send_b.at[peer], recv_b.at[me_c], b_send, b_recv, {"chan": peer}).start()

    send_b[me_c] = reduced(me_c)
    pltpu.make_async_copy(send_b.at[me_c], recv_b.at[me_c], b_recv).start()
    pltpu.make_async_copy(recv_b, recv_b, b_recv).wait()
    total = recv_b[0].astype(jnp.float32)
    for c in range(1, chans):
        total += recv_b[c].astype(jnp.float32)
    dtap_o[...] = total[:8] * out_scale
    dpoint_o[...] = total[8] * in_scale

    sent = xs.at[:, pl.ds(0, planes * (chans - 1))]
    pltpu.make_async_copy(sent, sent, send_sem).wait()
    sent_g = gs.at[pl.ds(0, pairs * (chans - 1))]
    pltpu.make_async_copy(sent_g, sent_g, g_send).wait()
    pltpu.make_async_copy(da_v, da_o, da_sem).wait()
    sent_b = send_b.at[pl.ds(0, chans - 1)]
    pltpu.make_async_copy(sent_b, sent_b, b_send).wait()


def shards(acts, w_point, w_tap, grad_out):
    spaces = lax.axis_size("space")
    chans = lax.axis_size("chan")
    width, rows, cells = acts.shape
    planes = rows // chans
    channels = width * chans
    filters = w_tap.shape[2]
    in_cells = rows * spaces * H * W
    chunks = (planes // 2) * (cells // CHUNK)
    bf16, f32 = jnp.bfloat16, jnp.float32
    vmem = pl.BlockSpec(memory_space=pltpu.VMEM)
    own = filters // spaces
    out, da, d_tap, d_point = pl.pallas_call(
        functools.partial(kernel, spaces, chans, planes, 1.0 / math.sqrt(in_cells), 1.0 / math.sqrt(in_cells // 8)),
        out_shape=(
            jax.ShapeDtypeStruct((planes // 2, filters, cells // 4), bf16),
            jax.ShapeDtypeStruct((planes, channels, cells), bf16),
            jax.ShapeDtypeStruct((8, width, own), f32),
            jax.ShapeDtypeStruct((width, own), f32),
        ),
        in_specs=[pl.BlockSpec(memory_space=pl.ANY)] * 2 + [vmem] * 2,
        out_specs=(vmem, pl.BlockSpec(memory_space=pl.ANY), vmem, vmem),
        scratch_shapes=[
            pltpu.VMEM((cells // CHUNK, rows, width, CHUNK), bf16),
            pltpu.VMEM((rows // 2, width, cells // 4), bf16),
            pltpu.VMEM((2, width, rows, CHUNK), bf16),
            pltpu.VMEM((width, rows // 2, cells // 4), bf16),
            pltpu.VMEM((planes, channels, cells), bf16),
            pltpu.VMEM((chunks, 2, channels, CHUNK), bf16),
            pltpu.VMEM((planes // 2, filters, cells // 4), bf16),
            pltpu.VMEM((spaces, 9, channels, own), f32),
            pltpu.VMEM((spaces, 9, channels, own), f32),
            pltpu.VMEM((chans, 9, width, own), bf16),
            pltpu.VMEM((chans, 9, width, own), bf16),
            pltpu.VMEM((channels, 2 * CHUNK), bf16),
            pltpu.VMEM((2, 2, channels, BLOCK), bf16),
            pltpu.VMEM((channels, 2 * CHUNK), bf16),
            pltpu.VMEM((8 * channels, CHUNK // 4), bf16),
            pltpu.VMEM((BLOCK, BLOCK), bf16),
            pltpu.VMEM((BLOCK, BLOCK), bf16),
            pltpu.VMEM((filters, 8 * channels), bf16),
            pltpu.VMEM((channels, channels), bf16),
            pltpu.SemaphoreType.DMA((2,)),
            pltpu.SemaphoreType.DMA,
            pltpu.SemaphoreType.DMA,
            pltpu.SemaphoreType.DMA,
            pltpu.SemaphoreType.DMA,
            pltpu.SemaphoreType.DMA((chunks,)),
            pltpu.SemaphoreType.DMA,
            pltpu.SemaphoreType.DMA((max(spaces - 1, 1),)),
            pltpu.SemaphoreType.DMA((max(spaces - 1, 1),)),
            pltpu.SemaphoreType.DMA,
            pltpu.SemaphoreType.DMA,
        ],
        compiler_params=pltpu.CompilerParams(
            collective_id=0, has_side_effects=True, vmem_limit_bytes=58 * 2**20
        ),
        cost_estimate=pl.CostEstimate(flops=24 * 10**9, bytes_accessed=30 * 10**6, transcendentals=4 * 10**6),
    )(acts, grad_out, w_point, w_tap)
    return (jnp.transpose(out, (1, 0, 2)), jnp.transpose(da, (1, 0, 2)), d_point, d_tap)


def solution(mesh):
    placed = (P("chan", "space", None), P(), P(), P("chan", "space", None))
    return jax.shard_map(
        shards,
        mesh=mesh,
        in_specs=placed,
        out_specs=(
            P(None, ("space", "chan"), None),
            P(None, ("space", "chan"), None),
            P("chan", "space"),
            P(None, "chan", "space"),
        ),
        check_vma=False,
    )
```

```python
import functools
import math

import jax
import jax.numpy as jnp
from jax import lax
from jax.experimental import pallas as pl
from jax.experimental.pallas import tpu as pltpu
from jax.sharding import PartitionSpec as P

H = 64
W = 64
BLOCK = 8 * W
CHUNK = 2 * BLOCK
ROOT = math.sqrt(2.0 / math.pi)
CUBIC = 0.044715


def dot(a, b):
    return lax.dot_general(a, b, (((1,), (0,)), ((), ())), preferred_element_type=jnp.float32)


def dot_nt(a, b):
    return lax.dot_general(a, b, (((1,), (1,)), ((), ())), preferred_element_type=jnp.float32)


def tap_order(position):
    quarter = BLOCK // 4
    u = position // quarter
    rest = position % quarter
    i = rest // (W // 2)
    j = rest % (W // 2)
    return (2 * i + u // 2) * W + 2 * j + u % 2


def kernel(
    spaces, chans, planes, in_scale, out_scale,
    acts, grad_out, wp, wt,
    out_o, da_o, dtap_o, dpoint_o,
    xs, gs, stage, g_stage, da_v, da_p,
    recv, recvg, acc, recv_a, send_b, recv_b, taps, dtaps, grads, hid, order, back, wt_t, wp_t,
    load_sem, g_load, da_sem, send_sem, g_send, recv_sem, g_recv, a_send, a_recv, b_send, b_recv,
):
    me_s, me_c = lax.axis_index("space"), lax.axis_index("chan")
    width = acts.shape[0]
    pairs = planes // 2
    parts = acts.shape[2] // CHUNK

    def load(part, slot):
        lanes = pl.ds(pl.multiple_of(part * CHUNK, CHUNK), CHUNK)
        return pltpu.make_async_copy(acts.at[:, :, lanes], stage.at[slot], load_sem.at[slot])

    g_copy = pltpu.make_async_copy(grad_out, g_stage, g_load)
    g_copy.start()
    load(0, 0).start()

    def leave(part, slot):
        lanes = pl.ds(pl.multiple_of(part * CHUNK, CHUNK), CHUNK)
        return pltpu.make_async_copy(da_v.at[slot], da_o.at[:, :, lanes], da_sem.at[slot])

    def swap(src, dst):
        @pl.loop(0, src.shape[2] // 128)
        def _(lane):
            lanes = pl.ds(pl.multiple_of(lane * 128, 128), 128)
            for r in range(0, src.shape[1], 16):
                piece = src[:, r:r + 16, lanes].astype(jnp.float32)
                dst[r:r + 16, :, lanes] = jnp.swapaxes(piece, 0, 1).astype(jnp.bfloat16)

    out_cells = CHUNK // 4
    filters = acc.shape[3]

    barrier = pltpu.get_barrier_semaphore()
    for o in range(1, chans):
        pl.semaphore_signal(barrier, inc=1, device_id={"chan": lax.rem(me_c + o, chans)})
    for o in range(1, spaces):
        pl.semaphore_signal(barrier, inc=1, device_id={"space": lax.rem(me_s + o, spaces)})
    pl.semaphore_wait(barrier, chans + spaces - 2)

    mine = pl.ds(pl.multiple_of(me_c * width, width), width)

    def remote(src, dst, ssem, rsem, device):
        return pltpu.make_async_remote_copy(
            src_ref=src, dst_ref=dst, send_sem=ssem, recv_sem=rsem, device_id=device)

    def g_block(peer):
        return gs.at[pl.ds(peer * pairs, pairs)]

    def x_block(peer, k):
        return xs.at[k // pairs, pl.ds(peer * planes + 2 * (k % pairs), 2)]

    g_copy.wait()
    swap(g_stage, gs)
    pltpu.make_async_copy(g_block(me_c), recvg.at[:, mine], g_recv).start()

    @pl.loop(1, chans)
    def _(o):
        peer = lax.rem(me_c + o, chans)
        remote(g_block(peer), recvg.at[:, mine], g_send, g_recv, {"chan": peer}).start()

    @pl.loop(0, parts)
    def _(part):
        slot = part % 2

        @pl.when(part + 1 < parts)
        def _():
            load(part + 1, (part + 1) % 2).start()

        load(part, slot).wait()
        swap(stage.at[slot], xs.at[part])

        @pl.loop(0, pairs)
        def _(q):
            k = part * pairs + q
            pltpu.make_async_copy(x_block(me_c, k), recv.at[k, :, mine], recv_sem.at[k]).start()

            @pl.loop(1, chans)
            def _(o):
                peer = lax.rem(me_c + o, chans)
                remote(x_block(peer, k), recv.at[k, :, mine], send_sem, recv_sem.at[k], {"chan": peer}).start()

    acc[...] = jnp.zeros_like(acc)
    rows = lax.broadcasted_iota(jnp.int32, (BLOCK, BLOCK), 0)
    cols = lax.broadcasted_iota(jnp.int32, (BLOCK, BLOCK), 1)
    order[...] = jnp.where(rows == tap_order(cols), 1.0, 0.0).astype(jnp.bfloat16)
    back[...] = jnp.where(cols == tap_order(rows), 1.0, 0.0).astype(jnp.bfloat16)
    wp_t[...] = wp[...].astype(jnp.float32).T.astype(jnp.bfloat16)

    @pl.loop(0, 8)
    def _(t):
        wt_t[:, pl.ds(pl.multiple_of(t * wp.shape[0], 128), wp.shape[0])] = wt[t].astype(jnp.float32).T.astype(jnp.bfloat16)

    def add_term(slot, term):
        for s in range(spaces):
            acc[s, slot] += term[:, s * filters:(s + 1) * filters]

    pltpu.make_async_copy(recvg, recvg, g_recv).wait()

    @pl.loop(0, pairs * parts)
    def _(k):
        pltpu.make_async_copy(recv.at[k], recv.at[k], recv_sem.at[k]).wait()
        q, part = k % pairs, k // pairs
        quarter = BLOCK // 4
        for a in range(2):
            for h in range(2):
                moved = dot(recv[k, a, :, h * BLOCK:(h + 1) * BLOCK], order[...]).astype(jnp.bfloat16)
                for u in range(4):
                    at = (4 * a + u) * out_cells + h * quarter
                    taps[:, at:at + quarter] = moved[:, u * quarter:(u + 1) * quarter]
        g_lanes = pl.ds(pl.multiple_of(part * out_cells, out_cells), out_cells)
        g = recvg[q, :, g_lanes]
        for t in range(8):
            here = slice(t * out_cells, (t + 1) * out_cells)
            x = taps[:, here]
            pre = dot(wp_t[...], x)
            dh = dot(wt[t], g)
            square = pre * pre
            th = jnp.tanh(ROOT * pre * (1.0 + CUBIC * square))
            half = 0.5 * (1.0 + th)
            hidden = (pre * half).astype(jnp.bfloat16)
            slope = half + (0.5 * ROOT) * pre * (1.0 - th * th) * (1.0 + 3.0 * CUBIC * square)
            grad = (dh * slope).astype(jnp.bfloat16)
            hid[t * hidden.shape[0]:(t + 1) * hidden.shape[0], :] = hidden
            grads[:, here] = grad
            add_term(t, dot_nt(hidden, g))
            d_in = dot(wp[...], grad).astype(jnp.bfloat16)
            for h in range(2):
                dtaps[t // 4, h, :, (t % 4) * quarter:(t % 4 + 1) * quarter] = d_in[:, h * quarter:(h + 1) * quarter]
        add_term(8, dot_nt(taps[...], grads[...]))
        out_o[q, :, g_lanes] = dot(wt_t[...], hid[...]).astype(jnp.bfloat16)
        for a in range(2):
            for h in range(2):
                da_p[2 * q + a, :, h * BLOCK:(h + 1) * BLOCK] = dot(dtaps[a, h], back[...]).astype(jnp.bfloat16)

        @pl.when(q == pairs - 1)
        def _():
            slot = part % 2

            @pl.when(part >= 2)
            def _():
                leave(part - 2, slot).wait()

            @pl.loop(0, CHUNK // 128)
            def _(lane):
                lanes = pl.ds(pl.multiple_of(lane * 128, 128), 128)
                for c in range(0, da_p.shape[1], 64):
                    piece = da_p[:, c:c + 64, lanes].astype(jnp.float32)
                    da_v[slot, c:c + 64, :, lanes] = jnp.swapaxes(piece, 0, 1).astype(jnp.bfloat16)

            leave(part, slot).start()

    copies = []
    for o in range(1, spaces):
        other = lax.rem(me_s + o, spaces)
        copy = remote(acc.at[other], recv_a.at[me_s], a_send.at[o - 1], a_recv.at[o - 1], {"space": other})
        copy.start()
        copies.append(copy)
    for copy in copies:
        copy.wait()

    def reduced(c):
        at = pl.ds(pl.multiple_of(c * width, width), width)
        total = acc[me_s, :, at, :]
        for o in range(1, spaces):
            total += recv_a[lax.rem(me_s + o, spaces), :, at, :]
        return total.astype(jnp.bfloat16)

    @pl.loop(1, chans)
    def _(o):
        peer = lax.rem(me_c + o, chans)
        send_b[peer] = reduced(peer)
        remote(send_b.at[peer], recv_b.at[me_c], b_send, b_recv, {"chan": peer}).start()

    send_b[me_c] = reduced(me_c)
    pltpu.make_async_copy(send_b.at[me_c], recv_b.at[me_c], b_recv).start()
    pltpu.make_async_copy(recv_b, recv_b, b_recv).wait()
    total = recv_b[0].astype(jnp.float32)
    for c in range(1, chans):
        total += recv_b[c].astype(jnp.float32)
    dtap_o[...] = total[:8] * out_scale
    dpoint_o[...] = total[8] * in_scale

    sent = xs.at[:, pl.ds(0, planes * (chans - 1))]
    pltpu.make_async_copy(sent, sent, send_sem).wait()
    sent_g = gs.at[pl.ds(0, pairs * (chans - 1))]
    pltpu.make_async_copy(sent_g, sent_g, g_send).wait()
    for part in range(max(parts - 2, 0), parts):
        leave(part, part % 2).wait()
    sent_b = send_b.at[pl.ds(0, chans - 1)]
    pltpu.make_async_copy(sent_b, sent_b, b_send).wait()


def shards(acts, w_point, w_tap, grad_out):
    spaces = lax.axis_size("space")
    chans = lax.axis_size("chan")
    width, rows, cells = acts.shape
    planes = rows // chans
    channels = width * chans
    filters = w_tap.shape[2]
    in_cells = rows * spaces * H * W
    chunks = (planes // 2) * (cells // CHUNK)
    bf16, f32 = jnp.bfloat16, jnp.float32
    vmem = pl.BlockSpec(memory_space=pltpu.VMEM)
    own = filters // spaces
    out, da, d_tap, d_point = pl.pallas_call(
        functools.partial(kernel, spaces, chans, planes, 1.0 / math.sqrt(in_cells), 1.0 / math.sqrt(in_cells // 8)),
        out_shape=(
            jax.ShapeDtypeStruct((planes // 2, filters, cells // 4), bf16),
            jax.ShapeDtypeStruct((channels, planes, cells), bf16),
            jax.ShapeDtypeStruct((8, width, own), f32),
            jax.ShapeDtypeStruct((width, own), f32),
        ),
        in_specs=[pl.BlockSpec(memory_space=pl.ANY)] * 2 + [vmem] * 2,
        out_specs=(vmem, pl.BlockSpec(memory_space=pl.ANY), vmem, vmem),
        scratch_shapes=[
            pltpu.VMEM((cells // CHUNK, rows, width, CHUNK), bf16),
            pltpu.VMEM((rows // 2, width, cells // 4), bf16),
            pltpu.VMEM((2, width, rows, CHUNK), bf16),
            pltpu.VMEM((width, rows // 2, cells // 4), bf16),
            pltpu.VMEM((2, channels, planes, CHUNK), bf16),
            pltpu.VMEM((planes, channels, CHUNK), bf16),
            pltpu.VMEM((chunks, 2, channels, CHUNK), bf16),
            pltpu.VMEM((planes // 2, filters, cells // 4), bf16),
            pltpu.VMEM((spaces, 9, channels, own), f32),
            pltpu.VMEM((spaces, 9, channels, own), f32),
            pltpu.VMEM((chans, 9, width, own), bf16),
            pltpu.VMEM((chans, 9, width, own), bf16),
            pltpu.VMEM((channels, 2 * CHUNK), bf16),
            pltpu.VMEM((2, 2, channels, BLOCK), bf16),
            pltpu.VMEM((channels, 2 * CHUNK), bf16),
            pltpu.VMEM((8 * channels, CHUNK // 4), bf16),
            pltpu.VMEM((BLOCK, BLOCK), bf16),
            pltpu.VMEM((BLOCK, BLOCK), bf16),
            pltpu.VMEM((filters, 8 * channels), bf16),
            pltpu.VMEM((channels, channels), bf16),
            pltpu.SemaphoreType.DMA((2,)),
            pltpu.SemaphoreType.DMA,
            pltpu.SemaphoreType.DMA((2,)),
            pltpu.SemaphoreType.DMA,
            pltpu.SemaphoreType.DMA,
            pltpu.SemaphoreType.DMA((chunks,)),
            pltpu.SemaphoreType.DMA,
            pltpu.SemaphoreType.DMA((max(spaces - 1, 1),)),
            pltpu.SemaphoreType.DMA((max(spaces - 1, 1),)),
            pltpu.SemaphoreType.DMA,
            pltpu.SemaphoreType.DMA,
        ],
        compiler_params=pltpu.CompilerParams(
            collective_id=0, has_side_effects=True, vmem_limit_bytes=58 * 2**20
        ),
        cost_estimate=pl.CostEstimate(flops=24 * 10**9, bytes_accessed=30 * 10**6, transcendentals=4 * 10**6),
    )(acts, grad_out, w_point, w_tap)
    return (jnp.transpose(out, (1, 0, 2)), da, d_point, d_tap)


def solution(mesh):
    placed = (P("chan", "space", None), P(), P(), P("chan", "space", None))
    return jax.shard_map(
        shards,
        mesh=mesh,
        in_specs=placed,
        out_specs=(
            P(None, ("space", "chan"), None),
            P(None, ("space", "chan"), None),
            P("chan", "space"),
            P(None, "chan", "space"),
        ),
        check_vma=False,
    )
```
